512 devices in a mesh: lat: 64 (over y_lo, z, core), lon: 8 (over y_hi, x).
Axes of the slice: x: 4, y: 4 (y_hi: 2, y_lo: 2; y = y_hi * 2 + y_lo), z: 16, core: 2. Of those that a mesh axis runs over, the one named last changes fastest.
Arguments:
- right_side: float32 [4, 4096, 7168], P(None, 'lat', 'lon'), may hold values from -8 to 8
- start: float32 [4, 4096, 7168], P(None, 'lat', 'lon'), may hold values from -8 to 8
- absorb: float32 [4, 4096, 7168], P(None, 'lat', 'lon'), may hold values from 0.05 to 1
- kappa_lat: float32 [4096, 7168], P('lat', 'lon'), may hold values from 0.2 to 5
- kappa_lon: float32 [4096, 7168], P('lat', 'lon'), may hold values from 0.2 to 5
Outputs:
- smoothed: float32 [4, 4096, 7168], P(None, 'lat', 'lon')
- residual: float32 [4, 4096, 7168], P(None, 'lat', 'lon')
The draws below stay inside these ranges and needn't reach their ends.
All inputs are finite; a program needn't handle non-finite values.
Results may differ from the reference program's by a relative error of at most 0.00002.
Values sent between devices are 32-bit elements; how exact they have to be, the bound alone decides.
A program may use at most 64 MiB of HBM per device.

```python
import math
import jax
import jax.numpy as jnp

LEV = 4
SWEEPS = 4
NLAT = 4096
NLON = 7168


def levels(own_key, shape, pieces, low, top_value):
    def one(position, blocks):
        steps = jax.random.uniform(jax.random.fold_in(jax.random.fold_in(own_key, 6), position), (blocks,), jnp.float32, low / len(pieces), top_value / len(pieces))
        return jnp.repeat(jnp.exp(steps), shape[position] // blocks).reshape((-1,) + (1,) * (len(shape) - position - 1))

    factor_of = one(*pieces[0])
    for cut in pieces[1:]:
        factor_of = factor_of * one(*cut)
    return factor_of


def centred(rng, dims, spread, reach, shards=(), kind=jnp.bfloat16):
    array = spread * jax.random.normal(rng, dims, jnp.float32)
    if shards:
        array = array * levels(rng, dims, shards, -0.22, 0.18)
    return jnp.clip(array, -reach, reach).astype(kind)


def setup_inputs(seed: int = 0) -> dict:
    streams_of = jax.random.split(jax.random.key(seed), 6)
    right_side = centred(streams_of[0], (LEV, NLAT, NLON), 1.0, 8.0, ((1, 64), (2, 8)), jnp.float32)
    start = centred(streams_of[1], (LEV, NLAT, NLON), 1.0, 8.0, ((1, 64), (2, 8)), jnp.float32)
    absorb = jnp.clip(jnp.exp(math.log(1.0) - 2.9957323 * jax.random.uniform(streams_of[2], (LEV, NLAT, NLON), jnp.float32) ** levels(streams_of[2], (LEV, NLAT, NLON), ((1, 64), (2, 8)), -0.2, 0.2)), 0.05, 1.0)
    kappa_lat = jnp.clip(jnp.exp(math.log(5.0) - 3.218876 * jax.random.uniform(streams_of[3], (NLAT, NLON), jnp.float32) ** levels(streams_of[3], (NLAT, NLON), ((0, 64), (1, 8)), -0.2, 0.2)), 0.2, 5.0)
    kappa_lon = jnp.clip(jnp.exp(math.log(5.0) - 3.218876 * jax.random.uniform(streams_of[4], (NLAT, NLON), jnp.float32) ** levels(streams_of[4], (NLAT, NLON), ((0, 64), (1, 8)), -0.2, 0.2)), 0.2, 5.0)
    return {"right_side": right_side, "start": start, "absorb": absorb, "kappa_lat": kappa_lat, "kappa_lon": kappa_lon}


THETA = 1.05
DELTA = 0.95


def neighbours(field):
    half = field.shape[2] // 2
    top = jnp.roll(field[:, :1], half, axis=2)
    bottom = jnp.roll(field[:, -1:], half, axis=2)
    north = jnp.concatenate([top, field[:, :-1]], axis=1)
    south = jnp.concatenate([field[:, 1:], bottom], axis=1)
    west = jnp.roll(field, 1, axis=2)
    east = jnp.roll(field, -1, axis=2)
    return north, south, west, east


def reference(right_side, start, absorb, kappa_lat, kappa_lon):
    kappas = jnp.stack([kappa_lat, kappa_lon])
    kap_n, kap_s, kap_w, kap_e = neighbours(kappas)
    c_north = 0.5 * (kappa_lat + kap_n[0])
    c_south = 0.5 * (kappa_lat + kap_s[0])
    c_west = 0.5 * (kappa_lon + kap_w[1])
    c_east = 0.5 * (kappa_lon + kap_e[1])
    diag = absorb + (c_north + c_south + c_west + c_east)

    def apply_op(field):
        north, south, west, east = neighbours(field)
        return diag * field - (c_north * north + c_south * south + c_west * west + c_east * east)

    sigma = THETA / DELTA
    rho = 1.0 / sigma
    state = start
    resid = right_side - apply_op(state)
    step_dir = resid / (THETA * diag)
    state = state + step_dir
    for sweep in range(SWEEPS - 1):
        resid = right_side - apply_op(state)
        rho_new = 1.0 / (2.0 * sigma - rho)
        step_dir = (rho_new * rho) * step_dir + (2.0 * rho_new / DELTA) * (resid / diag)
        state = state + step_dir
        rho = rho_new
    return state, right_side - apply_op(state)
```

```python
import functools

import jax
import jax.numpy as jnp
from jax import lax
from jax.experimental import pallas as pl
from jax.experimental.pallas import tpu as pltpu
from jax.sharding import PartitionSpec as P

SWEEPS = 4
THETA = 1.05
DELTA = 0.95

MESH = pl.DeviceIdType.MESH
LANES = 128
REACH = 5
START, KLAT, KLON, RIGHT, ABSORB = 0, 4, 5, 6, 10
PLANES = 14
NORTH, SOUTH = 0, 1
OWN, EXTRA = 16, 8


def sweep_factors():
    sigma = THETA / DELTA
    rho = 1.0 / sigma
    factors = []
    for _ in range(SWEEPS - 1):
        rho_new = 1.0 / (2.0 * sigma - rho)
        factors.append((rho_new * rho, 2.0 * rho_new / DELTA))
        rho = rho_new
    return factors


def lane_of(shape):
    return lax.broadcasted_iota(jnp.int32, shape, len(shape) - 1)


def from_west(left, here):
    axis = here.ndim - 1
    return pltpu.roll(jnp.where(lane_of(here.shape) == LANES - 1, left, here), 1, axis)


def from_east(right, here):
    axis = here.ndim - 1
    return pltpu.roll(jnp.where(lane_of(here.shape) == 0, right, here), LANES - 1, axis)


def each_tile(count, body):
    def step(t, carry):
        body(t)
        return carry

    lax.fori_loop(0, count, step, 0)


class Region:
    def __init__(self, field, other, gain, scaled, coeff, tiles):
        self.field, self.other, self.gain, self.scaled, self.coeff, self.tiles = field, other, gain, scaled, coeff, tiles

    def around(self, t):
        return lax.rem(t + self.tiles - 1, self.tiles), lax.rem(t + 1, self.tiles)

    def coupling(self, x, t, first, cn, cs, cw, ce):
        west, east = self.around(t)
        rows = pl.ds(first, 8)
        here = x[0:4, t, rows, :]
        total = cn * x[0:4, t, pl.ds(first - 1, 8), :] + cs * x[0:4, t, pl.ds(first + 1, 8), :]
        total += cw * from_west(x[0:4, west, rows, :], here) + ce * from_east(x[0:4, east, rows, :], here)
        return here, total

    def opening(self, starts):
        def tile(t):
            west, east = self.around(t)
            for first in starts:
                rows = pl.ds(first, 8)
                kap = self.field[KLAT, t, rows, :]
                cn = 0.5 * (kap + self.field[KLAT, t, pl.ds(first - 1, 8), :])
                cs = 0.5 * (kap + self.field[KLAT, t, pl.ds(first + 1, 8), :])
                kap = self.field[KLON, t, rows, :]
                cw = 0.5 * (kap + from_west(self.field[KLON, west, rows, :], kap))
                ce = 0.5 * (kap + from_east(self.field[KLON, east, rows, :], kap))
                for place, value in enumerate((cn, cs, cw, ce)):
                    self.coeff[place, t, rows, :] = value
                gain = 1.0 / (self.field[ABSORB : ABSORB + 4, t, rows, :] + (cn + cs + cw + ce))
                scaled = self.field[RIGHT : RIGHT + 4, t, rows, :] * gain
                self.gain[:, t, rows, :] = gain
                self.scaled[:, t, rows, :] = scaled
                here, total = self.coupling(self.field, t, first, cn, cs, cw, ce)
                self.other[:, t, rows, :] = here + (scaled - here + gain * total) * (1.0 / THETA)

        each_tile(self.tiles, tile)

    def sweep(self, now, before, starts, keep, push):
        def tile(t):
            for first in starts:
                rows = pl.ds(first, 8)
                cn, cs, cw, ce = (self.coeff[place, t, rows, :] for place in range(4))
                here, total = self.coupling(now, t, first, cn, cs, cw, ce)
                change = push * (self.scaled[:, t, rows, :] + self.gain[:, t, rows, :] * total)
                before[0:4, t, rows, :] = (1.0 + keep - push) * here - keep * before[0:4, t, rows, :] + change

        each_tile(self.tiles, tile)

    def closing(self, x, starts, smoothed, residual, targets):
        def tile(t):
            columns = pl.ds(pl.multiple_of(t * LANES, LANES), LANES)
            for first, target in zip(starts, targets):
                rows = pl.ds(first, 8)
                cn, cs, cw, ce = (self.coeff[place, t, rows, :] for place in range(4))
                here, total = self.coupling(x, t, first, cn, cs, cw, ce)
                diag = self.field[ABSORB : ABSORB + 4, t, rows, :] + (cn + cs + cw + ce)
                smoothed[:, pl.ds(target, 8), columns] = here
                residual[:, pl.ds(target, 8), columns] = self.field[RIGHT : RIGHT + 4, t, rows, :] - (diag * here - total)

        each_tile(self.tiles - 1, tile)

    def run(self, starts, ends, smoothed, residual, targets):
        self.opening(starts)
        now, before = self.other, self.field
        for keep, push in sweep_factors():
            self.sweep(now, before, starts, keep, push)
            now, before = before, now
        self.closing(now, ends, smoothed, residual, targets)


def flipped(block):
    axis = block.ndim - 2
    row = lax.broadcasted_iota(jnp.int32, block.shape, axis)
    block = pltpu.roll(block, 4, axis)
    block = jnp.where((row & 2) == 0, pltpu.roll(block, 6, axis), pltpu.roll(block, 2, axis))
    return jnp.where((row & 1) == 0, pltpu.roll(block, 7, axis), pltpu.roll(block, 1, axis))


def kernel(
    bands, sectors, right_ref, start_ref, absorb_ref, klat_ref, klon_ref, smoothed, residual,
    field, other, gain, scaled, coeff,
    band_field, band_other, band_gain, band_scaled, band_coeff,
    to_west, to_east, east_in, west_in,
    load_sem, own_sem, row_send, row_recv, side_send, side_recv,
):
    rows = right_ref.shape[1]
    tiles = right_ref.shape[2] // LANES
    la, lo = lax.axis_index("lat"), lax.axis_index("lon")
    half = sectors // 2
    top, bottom = la == 0, la == bands - 1
    la_n = jnp.maximum(la - 1, 0)
    la_s = jnp.minimum(la + 1, bands - 1)
    lo_n = lo + jnp.where(top, half, 0)
    lo_s = lo + jnp.where(bottom, half, 0)

    def at(lat, lon):
        return (lat, lax.rem(lon + sectors, sectors))

    north, south, east, west = at(la_n, lo_n), at(la_s, lo_s), at(la, lo + 1), at(la, lo - 1)
    ne, nw, se, sw = at(la_n, lo_n + 1), at(la_n, lo_n - 1), at(la_s, lo_s + 1), at(la_s, lo_s - 1)

    barrier = pltpu.get_barrier_semaphore()
    for device in (north, south, east, west, ne, nw, se, sw):
        pl.semaphore_signal(barrier, inc=1, device_id=device, device_id_type=MESH)

    sources = ((start_ref, START, 4), (klat_ref, KLAT, 1), (klon_ref, KLON, 1), (right_ref, RIGHT, 4), (absorb_ref, ABSORB, 4))

    def load(t):
        columns = pl.ds(pl.multiple_of(t * LANES, LANES), LANES)
        for ref, plane, depth in sources:
            if depth == 1:
                src, dst = ref.at[:, columns], field.at[plane, t, pl.ds(8, rows), :]
            else:
                src, dst = ref.at[:, :, columns], field.at[plane : plane + 4, t, pl.ds(8, rows), :]
            pltpu.make_async_copy(src, dst, load_sem.at[t]).start()

    def loaded(t):
        whole = field.at[:, t, pl.ds(8, rows), :]
        pltpu.make_async_copy(whole, whole, load_sem.at[t]).wait()

    load(0)
    load(tiles - 1)
    lax.fori_loop(1, tiles - 1, lambda t, c: (load(t), c)[1], 0)
    pl.semaphore_wait(barrier, 8)

    def send_rows(way, device, band, from_top, into):
        def tile(t):
            columns = pl.ds(pl.multiple_of(t * LANES, LANES), LANES)
            for ref, plane, depth in sources:
                count = REACH if plane < KLON else REACH - 1
                first = 0 if from_top else rows - count
                group = 0 if plane < KLON else 1
                place = into if from_top else into + 8 - count
                if depth == 1:
                    src = ref.at[pl.ds(first, count), columns]
                    dst = band_field.at[band, plane, t, pl.ds(place, count), :]
                else:
                    src = ref.at[:, pl.ds(first, count), columns]
                    dst = band_field.at[band, plane : plane + 4, t, pl.ds(place, count), :]
                pltpu.make_async_remote_copy(
                    src_ref=src, dst_ref=dst, send_sem=row_send.at[way, group], recv_sem=row_recv.at[band, group],
                    device_id=device, device_id_type=MESH,
                ).start()

        each_tile(tiles, tile)

    pl.when(bottom)(lambda: send_rows(SOUTH, south, SOUTH, False, OWN))
    pl.when(jnp.logical_not(bottom))(lambda: send_rows(SOUTH, south, NORTH, False, 0))
    pl.when(top)(lambda: send_rows(NORTH, north, NORTH, True, 0))
    pl.when(jnp.logical_not(top))(lambda: send_rows(NORTH, north, SOUTH, True, OWN))

    loaded(0)
    loaded(tiles - 1)
    lane = lane_of((rows, LANES))
    for edge, kept, origin in ((0, to_west, 0), (tiles - 1, to_east, LANES - 8)):
        packed = jnp.zeros((rows, LANES), jnp.float32)
        for plane in range(PLANES):
            value = field[plane, edge, pl.ds(8, rows), :]
            shift = (8 * plane - origin) % LANES
            value = pltpu.roll(value, shift, 1) if shift else value
            packed = jnp.where((lane >= 8 * plane) & (lane < 8 * plane + 8), value, packed)
        kept[...] = packed

    def side(place, slot, src, dst, device):
        return pltpu.make_async_remote_copy(
            src_ref=src, dst_ref=dst, send_sem=side_send.at[place], recv_sem=side_recv.at[slot],
            device_id=device, device_id_type=MESH,
        )

    upper, lower = pl.ds(0, 8), pl.ds(8 + rows, 8)
    side(0, 1, to_east, west_in.at[pl.ds(8, rows), :], east).start()
    side(1, 0, to_west, east_in.at[pl.ds(8, rows), :], west).start()

    def corners(way, band, src, dst, right, left):
        side(2 + 2 * way, 3 + 2 * band, to_east.at[src, :], west_in.at[dst, :], right).start()
        side(3 + 2 * way, 2 + 2 * band, to_west.at[src, :], east_in.at[dst, :], left).start()

    first_rows, last_rows = pl.ds(0, 8), pl.ds(rows - 8, 8)
    pl.when(bottom)(lambda: corners(SOUTH, SOUTH, last_rows, lower, se, sw))
    pl.when(jnp.logical_not(bottom))(lambda: corners(SOUTH, NORTH, last_rows, upper, se, sw))
    pl.when(top)(lambda: corners(NORTH, NORTH, first_rows, upper, ne, nw))
    pl.when(jnp.logical_not(top))(lambda: corners(NORTH, SOUTH, first_rows, lower, ne, nw))

    lax.fori_loop(1, tiles - 1, lambda t, c: (loaded(t), c)[1], 0)
    copies = []
    for band, src, dst in ((NORTH, 8, EXTRA), (SOUTH, 8 + rows - OWN, 0)):
        copies.append(pltpu.make_async_copy(
            field.at[:, pl.ds(0, tiles), pl.ds(src, OWN), :],
            band_field.at[band, :, pl.ds(0, tiles), pl.ds(dst, OWN), :],
            own_sem.at[band],
        ))
        copies[-1].start()

    def unpacked(plane, right, left):
        back = (LANES - 8 * plane) % LANES
        right = pltpu.roll(right, back, 1) if back else right
        left = pltpu.roll(left, (LANES - 8 - 8 * plane) % LANES, 1)
        return jnp.where(lane_of(right.shape) < LANES // 2, right, left)

    middle = pl.ds(8, rows)
    for slot, box in ((0, east_in), (1, west_in)):
        pltpu.make_async_copy(box.at[middle, :], box.at[middle, :], side_recv.at[slot]).wait()
    for plane in range(PLANES):
        value = unpacked(plane, east_in[middle, :], west_in[middle, :])
        field[plane, tiles, middle, :] = value
        band_field[NORTH, plane, tiles, pl.ds(EXTRA, OWN), :] = value[:OWN]
        band_field[SOUTH, plane, tiles, pl.ds(0, OWN), :] = value[rows - OWN :]
    for copy in copies:
        copy.wait()

    inner = Region(field, other, gain, scaled, coeff, tiles + 1)
    inner.run(
        [12 + 8 * k for k in range(rows // 8 - 1)],
        [16 + 8 * k for k in range(rows // 8 - 2)],
        smoothed, residual,
        [8 + 8 * k for k in range(rows // 8 - 2)],
    )

    for band, turned, landing, box_rows, target in ((SOUTH, bottom, OWN, lower, rows - 8), (NORTH, top, 0, upper, 0)):
        for group, (planes, count) in enumerate(((slice(0, KLON), REACH), (slice(KLON, PLANES), REACH - 1))):
            got = band_field.at[band, planes, pl.ds(0, tiles), pl.ds(landing, count), :]
            pltpu.make_async_copy(got, got, row_recv.at[band, group]).wait()
        for slot, box in ((2 + 2 * band, east_in), (3 + 2 * band, west_in)):
            pltpu.make_async_copy(box.at[box_rows, :], box.at[box_rows, :], side_recv.at[slot]).wait()
        for plane in range(PLANES):
            band_field[band, plane, tiles, pl.ds(landing, 8), :] = unpacked(plane, east_in[box_rows, :], west_in[box_rows, :])

        @pl.when(turned)
        def _():
            def tile(t):
                block = band_field[band, :, t, pl.ds(landing, 8), :]
                band_field[band, :, t, pl.ds(landing, 8), :] = flipped(block)

            each_tile(tiles + 1, tile)

        edge = Region(
            band_field.at[band], band_other.at[band], band_gain.at[band], band_scaled.at[band], band_coeff.at[band], tiles + 1
        )
        edge.run([4, 12], [8], smoothed, residual, [target])

    for way in (SOUTH, NORTH):
        for group, (planes, count) in enumerate(((slice(0, KLON), REACH), (slice(KLON, PLANES), REACH - 1))):
            sent = band_field.at[way, planes, pl.ds(0, tiles), pl.ds(0, count), :]
            pltpu.make_async_copy(sent, sent, row_send.at[way, group]).wait()
        for place, box in ((2 + 2 * way, to_east), (3 + 2 * way, to_west)):
            pltpu.make_async_copy(box.at[first_rows, :], box.at[first_rows, :], side_send.at[place]).wait()
    for place, box in ((0, to_east), (1, to_west)):
        pltpu.make_async_copy(box, box, side_send.at[place]).wait()


def solution(mesh):
    bands, sectors = mesh.shape["lat"], mesh.shape["lon"]

    def on_device(right_side, start, absorb, kappa_lat, kappa_lon):
        levels, rows, columns = start.shape
        tiles = columns // LANES + 1
        deep = rows + 16

        def region(*shape):
            return [
                pltpu.VMEM(lead + (tiles,) + shape[-1:] + (LANES,), jnp.float32)
                for lead in ((*shape[:-1], PLANES),) + ((*shape[:-1], 4),) * 4
            ]

        out = pltpu.VMEM(start.shape, jnp.float32)
        return pl.pallas_call(
            functools.partial(kernel, bands, sectors),
            out_shape=(out, out),
            in_specs=[pl.BlockSpec(memory_space=pltpu.HBM)] * 5,
            out_specs=[pl.BlockSpec(memory_space=pltpu.VMEM)] * 2,
            scratch_shapes=region(deep) + region(2, OWN + EXTRA) + [
                pltpu.VMEM((rows, LANES), jnp.float32),
                pltpu.VMEM((rows, LANES), jnp.float32),
                pltpu.VMEM((deep, LANES), jnp.float32),
                pltpu.VMEM((deep, LANES), jnp.float32),
                pltpu.SemaphoreType.DMA((tiles - 1,)),
                pltpu.SemaphoreType.DMA((2,)),
                pltpu.SemaphoreType.DMA((2, 2)),
                pltpu.SemaphoreType.DMA((2, 2)),
                pltpu.SemaphoreType.DMA((6,)),
                pltpu.SemaphoreType.DMA((6,)),
            ],
            compiler_params=pltpu.CompilerParams(
                collective_id=0, has_side_effects=True, vmem_limit_bytes=62 * 1024 * 1024
            ),
        )(right_side, start, absorb, kappa_lat, kappa_lon)

    field = P(None, "lat", "lon")
    return jax.shard_map(
        on_device,
        mesh=mesh,
        in_specs=(field, field, field, P("lat", "lon"), P("lat", "lon")),
        out_specs=(field, field),
        check_vma=False,
    )
```

```python
import functools

import jax
import jax.numpy as jnp
from jax import lax
from jax.experimental import pallas as pl
from jax.experimental.pallas import tpu as pltpu
from jax.sharding import PartitionSpec as P

SWEEPS = 4
THETA = 1.05
DELTA = 0.95

INNER_CHUNK, INNER_UNROLL, INNER_END = 8, 2, 1
BAND_CHUNK, BAND_UNROLL, BAND_END = 8, 4, 7

MESH = pl.DeviceIdType.MESH
LANES = 128
REACH = 5
START, KLAT, KLON, RIGHT, ABSORB = 0, 4, 5, 6, 10
PLANES = 14
NORTH, SOUTH = 0, 1
OWN, EXTRA = 16, 8


def sweep_factors():
    sigma = THETA / DELTA
    rho = 1.0 / sigma
    factors = []
    for _ in range(SWEEPS - 1):
        rho_new = 1.0 / (2.0 * sigma - rho)
        factors.append((rho_new * rho, 2.0 * rho_new / DELTA))
        rho = rho_new
    return factors


def lane_of(shape):
    return lax.broadcasted_iota(jnp.int32, shape, len(shape) - 1)


def from_west(left, here):
    axis = here.ndim - 1
    return pltpu.roll(jnp.where(lane_of(here.shape) == LANES - 1, left, here), 1, axis)


def from_east(right, here):
    axis = here.ndim - 1
    return pltpu.roll(jnp.where(lane_of(here.shape) == 0, right, here), LANES - 1, axis)


def each_tile(count, body, unroll=1):
    def step(t, carry):
        body(t)
        return carry

    lax.fori_loop(0, count, step, 0, unroll=unroll)


def chunks(first, rows, most):
    return [(first + place, min(most, rows - place)) for place in range(0, rows, most)]


class Region:
    def __init__(self, field, other, gain, scaled, coeff, tiles, unroll, unroll_end):
        self.unroll, self.unroll_end = unroll, unroll_end
        self.field, self.other, self.gain, self.scaled, self.coeff, self.tiles = field, other, gain, scaled, coeff, tiles

    def around(self, t):
        return lax.rem(t + self.tiles - 1, self.tiles), lax.rem(t + 1, self.tiles)

    def coupling(self, x, t, first, count, cn, cs, cw, ce):
        west, east = self.around(t)
        rows = pl.ds(first, count)
        here = x[0:4, t, rows, :]
        total = cn * x[0:4, t, pl.ds(first - 1, count), :] + cs * x[0:4, t, pl.ds(first + 1, count), :]
        total += cw * from_west(x[0:4, west, rows, :], here) + ce * from_east(x[0:4, east, rows, :], here)
        return here, total

    def opening(self, starts):
        def tile(t):
            west, east = self.around(t)
            for first, count in starts:
                rows = pl.ds(first, count)
                kap = self.field[KLAT, t, rows, :]
                cn = 0.5 * (kap + self.field[KLAT, t, pl.ds(first - 1, count), :])
                cs = 0.5 * (kap + self.field[KLAT, t, pl.ds(first + 1, count), :])
                kap = self.field[KLON, t, rows, :]
                cw = 0.5 * (kap + from_west(self.field[KLON, west, rows, :], kap))
                ce = 0.5 * (kap + from_east(self.field[KLON, east, rows, :], kap))
                for place, value in enumerate((cn, cs, cw, ce)):
                    self.coeff[place, t, rows, :] = value
                gain = 1.0 / (self.field[ABSORB : ABSORB + 4, t, rows, :] + (cn + cs + cw + ce))
                scaled = self.field[RIGHT : RIGHT + 4, t, rows, :] * gain
                self.gain[:, t, rows, :] = gain
                self.scaled[:, t, rows, :] = scaled
                here, total = self.coupling(self.field, t, first, count, cn, cs, cw, ce)
                self.other[:, t, rows, :] = here + (scaled - here + gain * total) * (1.0 / THETA)

        each_tile(self.tiles, tile, self.unroll)

    def sweep(self, now, before, starts, keep, push):
        def tile(t):
            for first, count in starts:
                rows = pl.ds(first, count)
                cn, cs, cw, ce = (self.coeff[place, t, rows, :] for place in range(4))
                here, total = self.coupling(now, t, first, count, cn, cs, cw, ce)
                change = push * (self.scaled[:, t, rows, :] + self.gain[:, t, rows, :] * total)
                before[0:4, t, rows, :] = (1.0 + keep - push) * here - keep * before[0:4, t, rows, :] + change

        each_tile(self.tiles, tile, self.unroll)

    def closing(self, x, starts, smoothed, residual, targets):
        def tile(t):
            columns = pl.ds(pl.multiple_of(t * LANES, LANES), LANES)
            for (first, count), target in zip(starts, targets):
                rows = pl.ds(first, count)
                cn, cs, cw, ce = (self.coeff[place, t, rows, :] for place in range(4))
                here, total = self.coupling(x, t, first, count, cn, cs, cw, ce)
                diag = self.field[ABSORB : ABSORB + 4, t, rows, :] + (cn + cs + cw + ce)
                smoothed[:, pl.ds(target, count), columns] = here
                residual[:, pl.ds(target, count), columns] = self.field[RIGHT : RIGHT + 4, t, rows, :] - (diag * here - total)

        each_tile(self.tiles - 1, tile, self.unroll_end)

    def run(self, starts, ends, smoothed, residual, targets):
        self.opening(starts)
        now, before = self.other, self.field
        for keep, push in sweep_factors():
            self.sweep(now, before, starts, keep, push)
            now, before = before, now
        self.closing(now, ends, smoothed, residual, targets)


def flipped(block):
    axis = block.ndim - 2
    row = lax.broadcasted_iota(jnp.int32, block.shape, axis)
    block = pltpu.roll(block, 4, axis)
    block = jnp.where((row & 2) == 0, pltpu.roll(block, 6, axis), pltpu.roll(block, 2, axis))
    return jnp.where((row & 1) == 0, pltpu.roll(block, 7, axis), pltpu.roll(block, 1, axis))


def kernel(
    bands, sectors, right_ref, start_ref, absorb_ref, klat_ref, klon_ref, smoothed, residual,
    field, other, gain, scaled, coeff,
    band_field, band_other, band_gain, band_scaled, band_coeff,
    rows_in, to_west, to_east, east_in, west_in,
    load_sem, own_sem, row_send, row_recv, side_send, side_recv, north_in,
):
    rows = right_ref.shape[1]
    tiles = right_ref.shape[2] // LANES
    la, lo = lax.axis_index("lat"), lax.axis_index("lon")
    half = sectors // 2
    top, bottom = la == 0, la == bands - 1
    la_n = jnp.maximum(la - 1, 0)
    la_s = jnp.minimum(la + 1, bands - 1)
    lo_n = lo + jnp.where(top, half, 0)
    lo_s = lo + jnp.where(bottom, half, 0)

    def at(lat, lon):
        return (lat, lax.rem(lon + sectors, sectors))

    north, south, east, west = at(la_n, lo_n), at(la_s, lo_s), at(la, lo + 1), at(la, lo - 1)
    ne, nw, se, sw = at(la_n, lo_n + 1), at(la_n, lo_n - 1), at(la_s, lo_s + 1), at(la_s, lo_s - 1)

    seam = bands // 2
    above_seam, at_seam = la == seam - 1, la == seam
    barrier = pltpu.get_barrier_semaphore()

    def tell(semaphore, *devices):
        for device in devices:
            pl.semaphore_signal(semaphore, inc=1, device_id=device, device_id_type=MESH)

    tell(barrier, north, ne, nw, east, west)
    pl.when(jnp.logical_not(above_seam))(lambda: tell(barrier, south, se, sw))

    sources = ((start_ref, START, 4), (klat_ref, KLAT, 1), (klon_ref, KLON, 1), (right_ref, RIGHT, 4), (absorb_ref, ABSORB, 4))

    def load(t):
        columns = pl.ds(pl.multiple_of(t * LANES, LANES), LANES)
        for ref, plane, depth in sources:
            if depth == 1:
                src, dst = ref.at[:, columns], field.at[plane, t, pl.ds(8, rows), :]
            else:
                src, dst = ref.at[:, :, columns], field.at[plane : plane + 4, t, pl.ds(8, rows), :]
            pltpu.make_async_copy(src, dst, load_sem.at[t]).start()

    def loaded(t):
        whole = field.at[:, t, pl.ds(8, rows), :]
        pltpu.make_async_copy(whole, whole, load_sem.at[t]).wait()

    load(0)
    load(tiles - 1)
    lax.fori_loop(1, tiles - 1, lambda t, c: (load(t), c)[1], 0)
    pl.semaphore_wait(barrier, jnp.where(at_seam, 5, 8))

    def send_rows(way, device, band, from_top):
        for ref, plane, depth in sources:
            count = REACH if plane < KLON else REACH - 1
            first = 0 if from_top else rows - count
            group = 0 if plane < KLON else 1
            place = pl.ds(0 if from_top else 8 - count, count)
            if depth == 1:
                src, dst = ref.at[pl.ds(first, count), :], rows_in.at[band, plane, place, :]
            else:
                src, dst = ref.at[:, pl.ds(first, count), :], rows_in.at[band, plane : plane + 4, place, :]
            pltpu.make_async_remote_copy(
                src_ref=src, dst_ref=dst, send_sem=row_send.at[way, group], recv_sem=row_recv.at[band, group],
                device_id=device, device_id_type=MESH,
            ).start()

    band_s, band_n = jnp.where(bottom, SOUTH, NORTH), jnp.where(top, NORTH, SOUTH)
    pl.when(above_seam)(lambda: tell(north_in, south, se, sw))
    send_rows(SOUTH, south, band_s, False)

    pl.when(jnp.logical_not(at_seam))(lambda: send_rows(NORTH, north, band_n, True))

    loaded(0)
    loaded(tiles - 1)
    lane = lane_of((rows, LANES))
    for edge, kept, origin in ((0, to_west, 0), (tiles - 1, to_east, LANES - 8)):
        packed = jnp.zeros((rows, LANES), jnp.float32)
        for plane in range(PLANES):
            value = field[plane, edge, pl.ds(8, rows), :]
            shift = (8 * plane - origin) % LANES
            value = pltpu.roll(value, shift, 1) if shift else value
            packed = jnp.where((lane >= 8 * plane) & (lane < 8 * plane + 8), value, packed)
        kept[...] = packed

    def side(place, slot, src, dst, device):
        return pltpu.make_async_remote_copy(
            src_ref=src, dst_ref=dst, send_sem=side_send.at[place], recv_sem=side_recv.at[slot],
            device_id=device, device_id_type=MESH,
        )

    upper, lower = pl.ds(0, 8), pl.ds(8 + rows, 8)
    side(0, 1, to_east, west_in.at[pl.ds(8, rows), :], east).start()
    side(1, 0, to_west, east_in.at[pl.ds(8, rows), :], west).start()

    def corners(way, band, src, dst, right, left):
        side(2 + 2 * way, 3 + 2 * band, to_east.at[src, :], west_in.at[dst, :], right).start()
        side(3 + 2 * way, 2 + 2 * band, to_west.at[src, :], east_in.at[dst, :], left).start()

    first_rows, last_rows = pl.ds(0, 8), pl.ds(rows - 8, 8)
    def corners(way, band, src, right, left):
        dst = pl.ds(pl.multiple_of(band * (8 + rows), 8), 8)
        side(2 + 2 * way, 3 + 2 * band, to_east.at[src, :], west_in.at[dst, :], right).start()
        side(3 + 2 * way, 2 + 2 * band, to_west.at[src, :], east_in.at[dst, :], left).start()

    corners(SOUTH, band_s, last_rows, se, sw)
    pl.when(jnp.logical_not(at_seam))(lambda: corners(NORTH, band_n, first_rows, ne, nw))
    lax.fori_loop(1, tiles - 1, lambda t, c: (loaded(t), c)[1], 0)
    copies = []
    for band, src, dst in ((NORTH, 8, EXTRA), (SOUTH, 8 + rows - OWN, 0)):
        copies.append(pltpu.make_async_copy(
            field.at[:, pl.ds(0, tiles), pl.ds(src, OWN), :],
            band_field.at[band, :, pl.ds(0, tiles), pl.ds(dst, OWN), :],
            own_sem.at[band],
        ))
        copies[-1].start()

    def unpacked(plane, right, left):
        back = (LANES - 8 * plane) % LANES
        right = pltpu.roll(right, back, 1) if back else right
        left = pltpu.roll(left, (LANES - 8 - 8 * plane) % LANES, 1)
        return jnp.where(lane_of(right.shape) < LANES // 2, right, left)

    middle = pl.ds(8, rows)
    for slot, box in ((0, east_in), (1, west_in)):
        pltpu.make_async_copy(box.at[middle, :], box.at[middle, :], side_recv.at[slot]).wait()
    for plane in range(PLANES):
        value = unpacked(plane, east_in[middle, :], west_in[middle, :])
        field[plane, tiles, middle, :] = value
        band_field[NORTH, plane, tiles, pl.ds(EXTRA, OWN), :] = value[:OWN]
        band_field[SOUTH, plane, tiles, pl.ds(0, OWN), :] = value[rows - OWN :]
    for copy in copies:
        copy.wait()

    inner = Region(field, other, gain, scaled, coeff, tiles + 1, INNER_UNROLL, INNER_END)
    inner.run(
        chunks(12, rows - 8, INNER_CHUNK),
        chunks(16, rows - 16, INNER_CHUNK),
        smoothed, residual,
        [first - 8 for first, _ in chunks(16, rows - 16, INNER_CHUNK)],
    )

    for band, turned, landing, box_rows, target in ((SOUTH, bottom, OWN, lower, rows - 8), (NORTH, top, 0, upper, 0)):
        if band == NORTH:

            @pl.when(at_seam)
            def _():
                pl.semaphore_wait(north_in, 3)
                send_rows(NORTH, north, band_n, True)
                corners(NORTH, band_n, first_rows, ne, nw)

        for group, (planes, count) in enumerate(((slice(0, KLON), REACH), (slice(KLON, PLANES), REACH - 1))):
            got = rows_in.at[band, planes, pl.ds(0, count), :]
            pltpu.make_async_copy(got, got, row_recv.at[band, group]).wait()
        for slot, box in ((2 + 2 * band, east_in), (3 + 2 * band, west_in)):
            pltpu.make_async_copy(box.at[box_rows, :], box.at[box_rows, :], side_recv.at[slot]).wait()
        for plane in range(PLANES):
            band_field[band, plane, tiles, pl.ds(landing, 8), :] = unpacked(plane, east_in[box_rows, :], west_in[box_rows, :])

        def settle(order):
            def tile(t):
                columns = pl.ds(pl.multiple_of(t * LANES, LANES), LANES)
                band_field[band, :, t, pl.ds(landing, 8), :] = order(rows_in[band, :, :, columns])

            each_tile(tiles, tile)

        @pl.when(turned)
        def _():
            settle(flipped)
            block = band_field[band, :, tiles, pl.ds(landing, 8), :]
            band_field[band, :, tiles, pl.ds(landing, 8), :] = flipped(block)

        @pl.when(jnp.logical_not(turned))
        def _():
            settle(lambda block: block)

        edge = Region(
            band_field.at[band], band_other.at[band], band_gain.at[band], band_scaled.at[band], band_coeff.at[band], tiles + 1, BAND_UNROLL, BAND_END
        )
        edge.run(chunks(4, 16, BAND_CHUNK), [(8, 8)], smoothed, residual, [target])

    for way in (SOUTH, NORTH):
        for group, (planes, count) in enumerate(((slice(0, KLON), REACH), (slice(KLON, PLANES), REACH - 1))):
            sent = rows_in.at[way, planes, pl.ds(0, count), :]
            pltpu.make_async_copy(sent, sent, row_send.at[way, group]).wait()
        for place, box in ((2 + 2 * way, to_east), (3 + 2 * way, to_west)):
            pltpu.make_async_copy(box.at[first_rows, :], box.at[first_rows, :], side_send.at[place]).wait()
    for place, box in ((0, to_east), (1, to_west)):
        pltpu.make_async_copy(box, box, side_send.at[place]).wait()


def solution(mesh):
    bands, sectors = mesh.shape["lat"], mesh.shape["lon"]

    def on_device(right_side, start, absorb, kappa_lat, kappa_lon):
        levels, rows, columns = start.shape
        tiles = columns // LANES + 1
        deep = rows + 16

        def region(*shape):
            return [
                pltpu.VMEM(lead + (tiles,) + shape[-1:] + (LANES,), jnp.float32)
                for lead in ((*shape[:-1], PLANES),) + ((*shape[:-1], 4),) * 4
            ]

        out = pltpu.VMEM(start.shape, jnp.float32)
        return pl.pallas_call(
            functools.partial(kernel, bands, sectors),
            out_shape=(out, out),
            in_specs=[pl.BlockSpec(memory_space=pltpu.HBM)] * 5,
            out_specs=[pl.BlockSpec(memory_space=pltpu.VMEM)] * 2,
            scratch_shapes=region(deep) + region(2, OWN + EXTRA) + [
                pltpu.VMEM((2, PLANES, 8, columns), jnp.float32),
                pltpu.VMEM((rows, LANES), jnp.float32),
                pltpu.VMEM((rows, LANES), jnp.float32),
                pltpu.VMEM((deep, LANES), jnp.float32),
                pltpu.VMEM((deep, LANES), jnp.float32),
                pltpu.SemaphoreType.DMA((tiles - 1,)),
                pltpu.SemaphoreType.DMA((2,)),
                pltpu.SemaphoreType.DMA((2, 2)),
                pltpu.SemaphoreType.DMA((2, 2)),
                pltpu.SemaphoreType.DMA((6,)),
                pltpu.SemaphoreType.DMA((6,)),
                pltpu.SemaphoreType.REGULAR,
            ],
            compiler_params=pltpu.CompilerParams(
                collective_id=0, has_side_effects=True, vmem_limit_bytes=62 * 1024 * 1024
            ),
        )(right_side, start, absorb, kappa_lat, kappa_lon)

    field = P(None, "lat", "lon")
    return jax.shard_map(
        on_device,
        mesh=mesh,
        in_specs=(field, field, field, P("lat", "lon"), P("lat", "lon")),
        out_specs=(field, field),
        check_vma=False,
    )
```

```python
import functools

import jax
import jax.numpy as jnp
from jax import lax
from jax.experimental import pallas as pl
from jax.experimental.pallas import tpu as pltpu
from jax.sharding import PartitionSpec as P

SWEEPS = 4
THETA = 1.05
DELTA = 0.95

INNER_CHUNK, INNER_UNROLL, INNER_END = 8, 1, 1
BAND_CHUNK, BAND_UNROLL, BAND_END = 8, 8, 7

MESH = pl.DeviceIdType.MESH
LANES = 128
REACH = 5
START, KLAT, KLON, RIGHT, ABSORB = 0, 4, 5, 6, 10
PLANES = 14
NORTH, SOUTH = 0, 1
OWN, EXTRA = 16, 8


def sweep_factors():
    sigma = THETA / DELTA
    rho = 1.0 / sigma
    factors = []
    for _ in range(SWEEPS - 1):
        rho_new = 1.0 / (2.0 * sigma - rho)
        factors.append((rho_new * rho, 2.0 * rho_new / DELTA))
        rho = rho_new
    return factors


def lane_of(shape):
    return lax.broadcasted_iota(jnp.int32, shape, len(shape) - 1)


def from_west(left, here):
    axis = here.ndim - 1
    return pltpu.roll(jnp.where(lane_of(here.shape) == LANES - 1, left, here), 1, axis)


def from_east(right, here):
    axis = here.ndim - 1
    return pltpu.roll(jnp.where(lane_of(here.shape) == 0, right, here), LANES - 1, axis)


def each_tile(count, body, unroll=1):
    def step(t, carry):
        body(t)
        return carry

    lax.fori_loop(0, count, step, 0, unroll=unroll)


def chunks(first, rows, most):
    return [(first + place, min(most, rows - place)) for place in range(0, rows, most)]


class Region:
    def __init__(self, field, other, gain, scaled, coeff, tiles, unroll, unroll_end):
        self.unroll, self.unroll_end = unroll, unroll_end
        self.field, self.other, self.gain, self.scaled, self.coeff, self.tiles = field, other, gain, scaled, coeff, tiles

    def around(self, t):
        return lax.rem(t + self.tiles - 1, self.tiles), lax.rem(t + 1, self.tiles)

    def coupling(self, x, t, first, count, cn, cs, cw, ce):
        west, east = self.around(t)
        rows = pl.ds(first, count)
        here = x[0:4, t, rows, :]
        total = cn * x[0:4, t, pl.ds(first - 1, count), :] + cs * x[0:4, t, pl.ds(first + 1, count), :]
        total += cw * from_west(x[0:4, west, rows, :], here) + ce * from_east(x[0:4, east, rows, :], here)
        return here, total

    def opening(self, starts):
        def tile(t):
            west, east = self.around(t)
            for first, count in starts:
                rows = pl.ds(first, count)
                kap = self.field[KLAT, t, rows, :]
                cn = 0.5 * (kap + self.field[KLAT, t, pl.ds(first - 1, count), :])
                cs = 0.5 * (kap + self.field[KLAT, t, pl.ds(first + 1, count), :])
                kap = self.field[KLON, t, rows, :]
                cw = 0.5 * (kap + from_west(self.field[KLON, west, rows, :], kap))
                ce = 0.5 * (kap + from_east(self.field[KLON, east, rows, :], kap))
                for place, value in enumerate((cn, cs, cw, ce)):
                    self.coeff[place, t, rows, :] = value
                gain = 1.0 / (self.field[ABSORB : ABSORB + 4, t, rows, :] + (cn + cs + cw + ce))
                scaled = self.field[RIGHT : RIGHT + 4, t, rows, :] * gain
                self.gain[:, t, rows, :] = gain
                self.scaled[:, t, rows, :] = scaled
                here, total = self.coupling(self.field, t, first, count, cn, cs, cw, ce)
                self.other[:, t, rows, :] = here + (scaled - here + gain * total) * (1.0 / THETA)

        each_tile(self.tiles, tile, self.unroll)

    def sweep(self, now, before, starts, keep, push):
        def tile(t):
            for first, count in starts:
                rows = pl.ds(first, count)
                cn, cs, cw, ce = (self.coeff[place, t, rows, :] for place in range(4))
                here, total = self.coupling(now, t, first, count, cn, cs, cw, ce)
                change = push * (self.scaled[:, t, rows, :] + self.gain[:, t, rows, :] * total)
                before[0:4, t, rows, :] = (1.0 + keep - push) * here - keep * before[0:4, t, rows, :] + change

        each_tile(self.tiles, tile, self.unroll)

    def finished(self, x, t, first, count):
        rows = pl.ds(first, count)
        cn, cs, cw, ce = (self.coeff[place, t, rows, :] for place in range(4))
        here, total = self.coupling(x, t, first, count, cn, cs, cw, ce)
        diag = self.field[ABSORB : ABSORB + 4, t, rows, :] + (cn + cs + cw + ce)
        return here, self.field[RIGHT : RIGHT + 4, t, rows, :] - (diag * here - total)

    def closing(self, x, starts, smoothed, residual, targets, written):
        def tile(t):
            columns = pl.ds(pl.multiple_of(t * LANES, LANES), LANES)
            for (first, count), target in zip(starts, targets):
                here, left = self.finished(x, t, first, count)
                smoothed[:, pl.ds(target, count), columns] = here
                residual[:, pl.ds(target, count), columns] = left

        each_tile(written, tile, self.unroll_end)

    def closing_sides(self, x, starts, smoothed, residual, targets, last):
        for t, column, outer in ((0, last, True), (2, 0, False)):
            columns = pl.ds(column * LANES, LANES)
            for (first, count), target in zip(starts, targets):
                near = lane_of((4, count, LANES)) < LANES // 2
                near = jnp.logical_not(near) if outer else near
                for ref, value in zip((smoothed, residual), self.finished(x, t, first, count)):
                    place = (slice(None), pl.ds(target, count), columns)
                    ref[place] = jnp.where(near, value, ref[place])

    def sweeps(self, starts):
        self.opening(starts)
        now, before = self.other, self.field
        for keep, push in sweep_factors():
            self.sweep(now, before, starts, keep, push)
            now, before = before, now
        return now


def flipped(block):
    axis = block.ndim - 2
    row = lax.broadcasted_iota(jnp.int32, block.shape, axis)
    block = pltpu.roll(block, 4, axis)
    block = jnp.where((row & 2) == 0, pltpu.roll(block, 6, axis), pltpu.roll(block, 2, axis))
    return jnp.where((row & 1) == 0, pltpu.roll(block, 7, axis), pltpu.roll(block, 1, axis))


def kernel(
    bands, sectors, right_ref, start_ref, absorb_ref, klat_ref, klon_ref, smoothed, residual,
    field, other, gain, scaled, coeff,
    band_field, band_other, band_gain, band_scaled, band_coeff,
    side_field, side_other, side_gain, side_scaled, side_coeff,
    rows_in, to_west, to_east, east_in, west_in,
    load_sem, own_sem, row_send, row_recv, side_send, side_recv, north_in,
):
    rows = right_ref.shape[1]
    tiles = right_ref.shape[2] // LANES
    la, lo = lax.axis_index("lat"), lax.axis_index("lon")
    half = sectors // 2
    top, bottom = la == 0, la == bands - 1
    la_n = jnp.maximum(la - 1, 0)
    la_s = jnp.minimum(la + 1, bands - 1)
    lo_n = lo + jnp.where(top, half, 0)
    lo_s = lo + jnp.where(bottom, half, 0)

    def at(lat, lon):
        return (lat, lax.rem(lon + sectors, sectors))

    north, south, east, west = at(la_n, lo_n), at(la_s, lo_s), at(la, lo + 1), at(la, lo - 1)
    ne, nw, se, sw = at(la_n, lo_n + 1), at(la_n, lo_n - 1), at(la_s, lo_s + 1), at(la_s, lo_s - 1)

    seam = bands // 2
    two_above, above_seam, at_seam = la == seam - 2, la == seam - 1, la == seam
    barrier = pltpu.get_barrier_semaphore()

    def tell(semaphore, *devices):
        for device in devices:
            pl.semaphore_signal(semaphore, inc=1, device_id=device, device_id_type=MESH)

    tell(barrier, north, ne, nw)
    pl.when(jnp.logical_not(above_seam))(lambda: tell(barrier, east, west))
    pl.when(jnp.logical_not(above_seam | two_above))(lambda: tell(barrier, south, se, sw))

    sources = ((start_ref, START, 4), (klat_ref, KLAT, 1), (klon_ref, KLON, 1), (right_ref, RIGHT, 4), (absorb_ref, ABSORB, 4))

    def load(t):
        columns = pl.ds(pl.multiple_of(t * LANES, LANES), LANES)
        for ref, plane, depth in sources:
            if depth == 1:
                src, dst = ref.at[:, columns], field.at[plane, t, pl.ds(8, rows), :]
            else:
                src, dst = ref.at[:, :, columns], field.at[plane : plane + 4, t, pl.ds(8, rows), :]
            pltpu.make_async_copy(src, dst, load_sem.at[t]).start()

    def loaded(t):
        whole = field.at[:, t, pl.ds(8, rows), :]
        pltpu.make_async_copy(whole, whole, load_sem.at[t]).wait()

    load(0)
    load(tiles - 1)
    lax.fori_loop(1, tiles - 1, lambda t, c: (load(t), c)[1], 0)
    pl.semaphore_wait(barrier, jnp.where(above_seam, 3, jnp.where(at_seam, 5, 8)))

    def send_rows(way, device, band, from_top):
        for ref, plane, depth in sources:
            count = REACH if plane < KLON else REACH - 1
            first = 0 if from_top else rows - count
            group = 0 if plane < KLON else 1
            place = pl.ds(0 if from_top else 8 - count, count)
            if depth == 1:
                src, dst = ref.at[pl.ds(first, count), :], rows_in.at[band, plane, place, :]
            else:
                src, dst = ref.at[:, pl.ds(first, count), :], rows_in.at[band, plane : plane + 4, place, :]
            pltpu.make_async_remote_copy(
                src_ref=src, dst_ref=dst, send_sem=row_send.at[way, group], recv_sem=row_recv.at[band, group],
                device_id=device, device_id_type=MESH,
            ).start()

    band_s, band_n = jnp.where(bottom, SOUTH, NORTH), jnp.where(top, NORTH, SOUTH)
    pl.when(above_seam)(lambda: tell(north_in, south, se, sw))
    pl.when(two_above)(lambda: tell(north_in, south))
    send_rows(SOUTH, south, band_s, False)

    pl.when(above_seam)(lambda: pl.semaphore_wait(north_in, 1))
    pl.when(jnp.logical_not(at_seam))(lambda: send_rows(NORTH, north, band_n, True))

    loaded(0)
    loaded(tiles - 1)
    lane = lane_of((rows, LANES))
    for edge, kept, origin in ((0, to_west, 0), (tiles - 1, to_east, LANES - 8)):
        packed = jnp.zeros((rows, LANES), jnp.float32)
        for plane in range(PLANES):
            value = field[plane, edge, pl.ds(8, rows), :]
            shift = (8 * plane - origin) % LANES
            value = pltpu.roll(value, shift, 1) if shift else value
            packed = jnp.where((lane >= 8 * plane) & (lane < 8 * plane + 8), value, packed)
        kept[...] = packed

    def side(place, slot, src, dst, device):
        return pltpu.make_async_remote_copy(
            src_ref=src, dst_ref=dst, send_sem=side_send.at[place], recv_sem=side_recv.at[slot],
            device_id=device, device_id_type=MESH,
        )

    upper, lower = pl.ds(0, 8), pl.ds(8 + rows, 8)
    side(0, 1, to_east, west_in.at[pl.ds(8, rows), :], east).start()
    side(1, 0, to_west, east_in.at[pl.ds(8, rows), :], west).start()

    first_rows, last_rows = pl.ds(0, 8), pl.ds(rows - 8, 8)
    def corners(way, band, src, right, left):
        dst = pl.ds(pl.multiple_of(band * (8 + rows), 8), 8)
        side(2 + 2 * way, 3 + 2 * band, to_east.at[src, :], west_in.at[dst, :], right).start()
        side(3 + 2 * way, 2 + 2 * band, to_west.at[src, :], east_in.at[dst, :], left).start()

    corners(SOUTH, band_s, last_rows, se, sw)
    pl.when(jnp.logical_not(at_seam))(lambda: corners(NORTH, band_n, first_rows, ne, nw))
    lax.fori_loop(1, tiles - 1, lambda t, c: (loaded(t), c)[1], 0)
    copies = []
    for band, src, dst in ((NORTH, 8, EXTRA), (SOUTH, 8 + rows - OWN, 0)):
        copies.append(pltpu.make_async_copy(
            field.at[:, pl.ds(0, tiles), pl.ds(src, OWN), :],
            band_field.at[band, :, pl.ds(0, tiles), pl.ds(dst, OWN), :],
            own_sem.at[band],
        ))
        copies[-1].start()
    for place, t in ((0, tiles - 1), (2, 0)):
        copies.append(pltpu.make_async_copy(
            field.at[:, t, pl.ds(8, rows), :], side_field.at[:, place, pl.ds(8, rows), :], own_sem.at[2 + place // 2]
        ))
        copies[-1].start()

    def unpacked(plane, right, left):
        back = (LANES - 8 * plane) % LANES
        right = pltpu.roll(right, back, 1) if back else right
        left = pltpu.roll(left, (LANES - 8 - 8 * plane) % LANES, 1)
        return jnp.where(lane_of(right.shape) < LANES // 2, right, left)

    for copy in copies:
        copy.wait()

    starts, ends = chunks(12, rows - 8, INNER_CHUNK), chunks(16, rows - 16, INNER_CHUNK)
    targets = [first - 8 for first, _ in ends]
    inner = Region(field, other, gain, scaled, coeff, tiles, INNER_UNROLL, INNER_END)
    inner.closing(inner.sweeps(starts), ends, smoothed, residual, targets, tiles)

    middle = pl.ds(8, rows)
    for slot, box in ((0, east_in), (1, west_in)):
        pltpu.make_async_copy(box.at[middle, :], box.at[middle, :], side_recv.at[slot]).wait()
    for plane in range(PLANES):
        value = unpacked(plane, east_in[middle, :], west_in[middle, :])
        side_field[plane, 1, middle, :] = value
        band_field[NORTH, plane, tiles, pl.ds(EXTRA, OWN), :] = value[:OWN]
        band_field[SOUTH, plane, tiles, pl.ds(0, OWN), :] = value[rows - OWN :]

    sides = Region(side_field, side_other, side_gain, side_scaled, side_coeff, 3, 3, 1)
    sides.closing_sides(sides.sweeps(starts), ends, smoothed, residual, targets, tiles - 1)

    for band, turned, landing, box_rows, target in ((SOUTH, bottom, OWN, lower, rows - 8), (NORTH, top, 0, upper, 0)):
        if band == NORTH:

            @pl.when(at_seam)
            def _():
                pl.semaphore_wait(north_in, 3)
                send_rows(NORTH, north, band_n, True)
                corners(NORTH, band_n, first_rows, ne, nw)

        for group, (planes, count) in enumerate(((slice(0, KLON), REACH), (slice(KLON, PLANES), REACH - 1))):
            got = rows_in.at[band, planes, pl.ds(0, count), :]
            pltpu.make_async_copy(got, got, row_recv.at[band, group]).wait()
        for slot, box in ((2 + 2 * band, east_in), (3 + 2 * band, west_in)):
            pltpu.make_async_copy(box.at[box_rows, :], box.at[box_rows, :], side_recv.at[slot]).wait()
        for plane in range(PLANES):
            band_field[band, plane, tiles, pl.ds(landing, 8), :] = unpacked(plane, east_in[box_rows, :], west_in[box_rows, :])

        def settle(order):
            def tile(t):
                columns = pl.ds(pl.multiple_of(t * LANES, LANES), LANES)
                band_field[band, :, t, pl.ds(landing, 8), :] = order(rows_in[band, :, :, columns])

            each_tile(tiles, tile)

        @pl.when(turned)
        def _():
            settle(flipped)
            block = band_field[band, :, tiles, pl.ds(landing, 8), :]
            band_field[band, :, tiles, pl.ds(landing, 8), :] = flipped(block)

        @pl.when(jnp.logical_not(turned))
        def _():
            settle(lambda block: block)

        edge = Region(
            band_field.at[band], band_other.at[band], band_gain.at[band], band_scaled.at[band], band_coeff.at[band], tiles + 1, BAND_UNROLL, BAND_END
        )
        edge.closing(edge.sweeps(chunks(4, OWN, BAND_CHUNK)), [(8, 8)], smoothed, residual, [target], tiles)

    for way in (SOUTH, NORTH):
        for group, (planes, count) in enumerate(((slice(0, KLON), REACH), (slice(KLON, PLANES), REACH - 1))):
            sent = rows_in.at[way, planes, pl.ds(0, count), :]
            pltpu.make_async_copy(sent, sent, row_send.at[way, group]).wait()
        for place, box in ((2 + 2 * way, to_east), (3 + 2 * way, to_west)):
            pltpu.make_async_copy(box.at[first_rows, :], box.at[first_rows, :], side_send.at[place]).wait()
    for place, box in ((0, to_east), (1, to_west)):
        pltpu.make_async_copy(box, box, side_send.at[place]).wait()


def solution(mesh):
    bands, sectors = mesh.shape["lat"], mesh.shape["lon"]

    def on_device(right_side, start, absorb, kappa_lat, kappa_lon):
        levels, rows, columns = start.shape
        tiles = columns // LANES + 1
        deep = rows + 16

        def region(tiles, *shape):
            return [
                pltpu.VMEM(lead + (tiles,) + shape[-1:] + (LANES,), jnp.float32)
                for lead in ((*shape[:-1], PLANES),) + ((*shape[:-1], 4),) * 4
            ]

        out = pltpu.VMEM(start.shape, jnp.float32)
        return pl.pallas_call(
            functools.partial(kernel, bands, sectors),
            out_shape=(out, out),
            in_specs=[pl.BlockSpec(memory_space=pltpu.HBM)] * 5,
            out_specs=[pl.BlockSpec(memory_space=pltpu.VMEM)] * 2,
            scratch_shapes=region(tiles - 1, deep) + region(tiles, 2, OWN + EXTRA) + region(3, deep) + [
                pltpu.VMEM((2, PLANES, 8, columns), jnp.float32),
                pltpu.VMEM((rows, LANES), jnp.float32),
                pltpu.VMEM((rows, LANES), jnp.float32),
                pltpu.VMEM((deep, LANES), jnp.float32),
                pltpu.VMEM((deep, LANES), jnp.float32),
                pltpu.SemaphoreType.DMA((tiles - 1,)),
                pltpu.SemaphoreType.DMA((4,)),
                pltpu.SemaphoreType.DMA((2, 2)),
                pltpu.SemaphoreType.DMA((2, 2)),
                pltpu.SemaphoreType.DMA((6,)),
                pltpu.SemaphoreType.DMA((6,)),
                pltpu.SemaphoreType.REGULAR,
            ],
            compiler_params=pltpu.CompilerParams(
                collective_id=0, has_side_effects=True, vmem_limit_bytes=62 * 1024 * 1024
            ),
        )(right_side, start, absorb, kappa_lat, kappa_lon)

    field = P(None, "lat", "lon")
    return jax.shard_map(
        on_device,
        mesh=mesh,
        in_specs=(field, field, field, P("lat", "lon"), P("lat", "lon")),
        out_specs=(field, field),
        check_vma=False,
    )
```

```python
import functools

import jax
import jax.numpy as jnp
from jax import lax
from jax.experimental import pallas as pl
from jax.experimental.pallas import tpu as pltpu
from jax.sharding import PartitionSpec as P

SWEEPS = 4
THETA = 1.05
DELTA = 0.95

INNER_CHUNK, INNER_UNROLL, INNER_END = 8, 1, 1
BAND_CHUNK, BAND_UNROLL, BAND_END = 8, 8, 7

MESH = pl.DeviceIdType.MESH
LANES = 128
REACH = 5
START, KLAT, KLON, RIGHT, ABSORB = 0, 4, 5, 6, 10
PLANES = 14
NORTH, SOUTH = 0, 1
OWN, EXTRA = 16, 8


def sweep_factors():
    sigma = THETA / DELTA
    rho = 1.0 / sigma
    factors = []
    for _ in range(SWEEPS - 1):
        rho_new = 1.0 / (2.0 * sigma - rho)
        factors.append((rho_new * rho, 2.0 * rho_new / DELTA))
        rho = rho_new
    return factors


def lane_of(shape):
    return lax.broadcasted_iota(jnp.int32, shape, len(shape) - 1)


def from_west(left, here):
    axis = here.ndim - 1
    return pltpu.roll(jnp.where(lane_of(here.shape) == LANES - 1, left, here), 1, axis)


def from_east(right, here):
    axis = here.ndim - 1
    return pltpu.roll(jnp.where(lane_of(here.shape) == 0, right, here), LANES - 1, axis)


def each_tile(count, body, unroll=1):
    def step(t, carry):
        body(t)
        return carry

    lax.fori_loop(0, count, step, 0, unroll=unroll)


def chunks(first, rows, most):
    return [(first + place, min(most, rows - place)) for place in range(0, rows, most)]


class Region:
    def __init__(self, field, other, gain, scaled, coeff, tiles, unroll, unroll_end):
        self.unroll, self.unroll_end = unroll, unroll_end
        self.field, self.other, self.gain, self.scaled, self.coeff, self.tiles = field, other, gain, scaled, coeff, tiles

    def around(self, t):
        return lax.rem(t + self.tiles - 1, self.tiles), lax.rem(t + 1, self.tiles)

    def coupling(self, x, t, first, count, cn, cs, cw, ce):
        west, east = self.around(t)
        rows = pl.ds(first, count)
        here = x[0:4, t, rows, :]
        total = cn * x[0:4, t, pl.ds(first - 1, count), :] + cs * x[0:4, t, pl.ds(first + 1, count), :]
        total += cw * from_west(x[0:4, west, rows, :], here) + ce * from_east(x[0:4, east, rows, :], here)
        return here, total

    def opening(self, starts):
        def tile(t):
            west, east = self.around(t)
            for first, count in starts:
                rows = pl.ds(first, count)
                kap = self.field[KLAT, t, rows, :]
                cn = 0.5 * (kap + self.field[KLAT, t, pl.ds(first - 1, count), :])
                cs = 0.5 * (kap + self.field[KLAT, t, pl.ds(first + 1, count), :])
                kap = self.field[KLON, t, rows, :]
                cw = 0.5 * (kap + from_west(self.field[KLON, west, rows, :], kap))
                ce = 0.5 * (kap + from_east(self.field[KLON, east, rows, :], kap))
                for place, value in enumerate((cn, cs, cw, ce)):
                    self.coeff[place, t, rows, :] = value
                gain = 1.0 / (self.field[ABSORB : ABSORB + 4, t, rows, :] + (cn + cs + cw + ce))
                scaled = self.field[RIGHT : RIGHT + 4, t, rows, :] * gain
                self.gain[:, t, rows, :] = gain
                self.scaled[:, t, rows, :] = scaled
                here, total = self.coupling(self.field, t, first, count, cn, cs, cw, ce)
                self.other[:, t, rows, :] = here + (scaled - here + gain * total) * (1.0 / THETA)

        each_tile(self.tiles, tile, self.unroll)

    def sweep(self, now, before, starts, keep, push):
        def tile(t):
            for first, count in starts:
                rows = pl.ds(first, count)
                cn, cs, cw, ce = (self.coeff[place, t, rows, :] for place in range(4))
                here, total = self.coupling(now, t, first, count, cn, cs, cw, ce)
                change = push * (self.scaled[:, t, rows, :] + self.gain[:, t, rows, :] * total)
                before[0:4, t, rows, :] = (1.0 + keep - push) * here - keep * before[0:4, t, rows, :] + change

        each_tile(self.tiles, tile, self.unroll)

    def finished(self, x, t, first, count):
        rows = pl.ds(first, count)
        cn, cs, cw, ce = (self.coeff[place, t, rows, :] for place in range(4))
        here, total = self.coupling(x, t, first, count, cn, cs, cw, ce)
        diag = self.field[ABSORB : ABSORB + 4, t, rows, :] + (cn + cs + cw + ce)
        return here, self.field[RIGHT : RIGHT + 4, t, rows, :] - (diag * here - total)

    def closing(self, x, starts, smoothed, residual, targets, written):
        def tile(t):
            columns = pl.ds(pl.multiple_of(t * LANES, LANES), LANES)
            for (first, count), target in zip(starts, targets):
                here, left = self.finished(x, t, first, count)
                smoothed[:, pl.ds(target, count), columns] = here
                residual[:, pl.ds(target, count), columns] = left

        each_tile(written, tile, self.unroll_end)

    def closing_sides(self, x, starts, smoothed, residual, targets, last):
        for t, column, outer in ((0, last, True), (2, 0, False)):
            columns = pl.ds(column * LANES, LANES)
            for (first, count), target in zip(starts, targets):
                near = lane_of((4, count, LANES)) < LANES // 2
                near = jnp.logical_not(near) if outer else near
                for ref, value in zip((smoothed, residual), self.finished(x, t, first, count)):
                    place = (slice(None), pl.ds(target, count), columns)
                    ref[place] = jnp.where(near, value, ref[place])

    def sweeps(self, starts):
        self.opening(starts)
        now, before = self.other, self.field
        for keep, push in sweep_factors():
            self.sweep(now, before, starts, keep, push)
            now, before = before, now
        return now


def flipped(block):
    axis = block.ndim - 2
    row = lax.broadcasted_iota(jnp.int32, block.shape, axis)
    block = pltpu.roll(block, 4, axis)
    block = jnp.where((row & 2) == 0, pltpu.roll(block, 6, axis), pltpu.roll(block, 2, axis))
    return jnp.where((row & 1) == 0, pltpu.roll(block, 7, axis), pltpu.roll(block, 1, axis))


def kernel(
    bands, sectors, right_ref, start_ref, absorb_ref, klat_ref, klon_ref, smoothed, residual,
    field, other, gain, scaled, coeff,
    band_field, band_other, band_gain, band_scaled, band_coeff,
    side_field, side_other, side_gain, side_scaled, side_coeff,
    rows_in, to_west, to_east, east_in, west_in,
    load_sem, own_sem, row_send, row_recv, side_send, side_recv, north_in,
):
    rows = right_ref.shape[1]
    tiles = right_ref.shape[2] // LANES
    la, lo = lax.axis_index("lat"), lax.axis_index("lon")
    half = sectors // 2
    top, bottom = la == 0, la == bands - 1
    la_n = jnp.maximum(la - 1, 0)
    la_s = jnp.minimum(la + 1, bands - 1)
    lo_n = lo + jnp.where(top, half, 0)
    lo_s = lo + jnp.where(bottom, half, 0)

    def at(lat, lon):
        return (lat, lax.rem(lon + sectors, sectors))

    north, south, east, west = at(la_n, lo_n), at(la_s, lo_s), at(la, lo + 1), at(la, lo - 1)
    ne, nw, se, sw = at(la_n, lo_n + 1), at(la_n, lo_n - 1), at(la_s, lo_s + 1), at(la_s, lo_s - 1)

    seam = bands // 2
    two_above, above_seam, at_seam = la == seam - 2, la == seam - 1, la == seam
    barrier = pltpu.get_barrier_semaphore()

    def tell(semaphore, *devices):
        for device in devices:
            pl.semaphore_signal(semaphore, inc=1, device_id=device, device_id_type=MESH)

    tell(barrier, north, ne, nw)
    pl.when(jnp.logical_not(above_seam))(lambda: tell(barrier, east, west))
    pl.when(jnp.logical_not(above_seam | two_above))(lambda: tell(barrier, south, se, sw))

    sources = ((start_ref, START, 4), (klat_ref, KLAT, 1), (klon_ref, KLON, 1), (right_ref, RIGHT, 4), (absorb_ref, ABSORB, 4))

    def load(t):
        columns = pl.ds(pl.multiple_of(t * LANES, LANES), LANES)
        for ref, plane, depth in sources:
            if depth == 1:
                src, dst = ref.at[:, columns], field.at[plane, t, pl.ds(8, rows), :]
            else:
                src, dst = ref.at[:, :, columns], field.at[plane : plane + 4, t, pl.ds(8, rows), :]
            pltpu.make_async_copy(src, dst, load_sem.at[t]).start()

    def loaded(t):
        whole = field.at[:, t, pl.ds(8, rows), :]
        pltpu.make_async_copy(whole, whole, load_sem.at[t]).wait()

    load(0)
    load(tiles - 1)
    lax.fori_loop(1, tiles - 1, lambda t, c: (load(t), c)[1], 0)

    def send_rows(way, device, band, from_top):
        for ref, plane, depth in sources:
            count = REACH if plane < KLON else REACH - 1
            first = 0 if from_top else rows - count
            group = 0 if plane < KLON else 1
            place = pl.ds(0 if from_top else 8 - count, count)
            if depth == 1:
                src, dst = ref.at[pl.ds(first, count), :], rows_in.at[band, plane, place, :]
            else:
                src, dst = ref.at[:, pl.ds(first, count), :], rows_in.at[band, plane : plane + 4, place, :]
            pltpu.make_async_remote_copy(
                src_ref=src, dst_ref=dst, send_sem=row_send.at[way, group], recv_sem=row_recv.at[band, group],
                device_id=device, device_id_type=MESH,
            ).start()

    band_s, band_n = jnp.where(bottom, SOUTH, NORTH), jnp.where(top, NORTH, SOUTH)

    @pl.when(above_seam)
    def _():
        pl.semaphore_wait(barrier, 3)
        tell(north_in, south, se, sw)
        send_rows(SOUTH, south, band_s, False)

    loaded(0)
    loaded(tiles - 1)
    lane = lane_of((rows, LANES))
    for edge, kept, origin in ((0, to_west, 0), (tiles - 1, to_east, LANES - 8)):
        packed = jnp.zeros((rows, LANES), jnp.float32)
        for plane in range(PLANES):
            value = field[plane, edge, pl.ds(8, rows), :]
            shift = (8 * plane - origin) % LANES
            value = pltpu.roll(value, shift, 1) if shift else value
            packed = jnp.where((lane >= 8 * plane) & (lane < 8 * plane + 8), value, packed)
        kept[...] = packed

    def side(place, slot, src, dst, device):
        return pltpu.make_async_remote_copy(
            src_ref=src, dst_ref=dst, send_sem=side_send.at[place], recv_sem=side_recv.at[slot],
            device_id=device, device_id_type=MESH,
        )

    upper, lower = pl.ds(0, 8), pl.ds(8 + rows, 8)
    first_rows, last_rows = pl.ds(0, 8), pl.ds(rows - 8, 8)

    def corners(way, band, src, right, left):
        dst = pl.ds(pl.multiple_of(band * (8 + rows), 8), 8)
        side(2 + 2 * way, 3 + 2 * band, to_east.at[src, :], west_in.at[dst, :], right).start()
        side(3 + 2 * way, 2 + 2 * band, to_west.at[src, :], east_in.at[dst, :], left).start()

    pl.when(above_seam)(lambda: corners(SOUTH, band_s, last_rows, se, sw))

    @pl.when(jnp.logical_not(above_seam))
    def _():
        pl.semaphore_wait(barrier, jnp.where(at_seam, 5, 8))

    pl.when(two_above)(lambda: tell(north_in, south))
    pl.when(above_seam)(lambda: pl.semaphore_wait(north_in, 1))

    side(0, 1, to_east, west_in.at[pl.ds(8, rows), :], east).start()
    side(1, 0, to_west, east_in.at[pl.ds(8, rows), :], west).start()

    pl.when(jnp.logical_not(above_seam))(lambda: corners(SOUTH, band_s, last_rows, se, sw))
    pl.when(jnp.logical_not(at_seam))(lambda: corners(NORTH, band_n, first_rows, ne, nw))
    pl.when(jnp.logical_not(above_seam))(lambda: send_rows(SOUTH, south, band_s, False))
    pl.when(jnp.logical_not(at_seam))(lambda: send_rows(NORTH, north, band_n, True))
    lax.fori_loop(1, tiles - 1, lambda t, c: (loaded(t), c)[1], 0)
    copies = []
    for band, src, dst in ((NORTH, 8, EXTRA), (SOUTH, 8 + rows - OWN, 0)):
        copies.append(pltpu.make_async_copy(
            field.at[:, pl.ds(0, tiles), pl.ds(src, OWN), :],
            band_field.at[band, :, pl.ds(0, tiles), pl.ds(dst, OWN), :],
            own_sem.at[band],
        ))
        copies[-1].start()
    for place, t in ((0, tiles - 1), (2, 0)):
        copies.append(pltpu.make_async_copy(
            field.at[:, t, pl.ds(8, rows), :], side_field.at[:, place, pl.ds(8, rows), :], own_sem.at[2 + place // 2]
        ))
        copies[-1].start()

    def unpacked(plane, right, left):
        back = (LANES - 8 * plane) % LANES
        right = pltpu.roll(right, back, 1) if back else right
        left = pltpu.roll(left, (LANES - 8 - 8 * plane) % LANES, 1)
        return jnp.where(lane_of(right.shape) < LANES // 2, right, left)

    for copy in copies:
        copy.wait()

    starts, ends = chunks(12, rows - 8, INNER_CHUNK), chunks(16, rows - 16, INNER_CHUNK)
    targets = [first - 8 for first, _ in ends]
    inner = Region(field, other, gain, scaled, coeff, tiles, INNER_UNROLL, INNER_END)
    inner.closing(inner.sweeps(starts), ends, smoothed, residual, targets, tiles)

    middle = pl.ds(8, rows)
    for slot, box in ((0, east_in), (1, west_in)):
        pltpu.make_async_copy(box.at[middle, :], box.at[middle, :], side_recv.at[slot]).wait()
    for plane in range(PLANES):
        value = unpacked(plane, east_in[middle, :], west_in[middle, :])
        side_field[plane, 1, middle, :] = value
        band_field[NORTH, plane, tiles, pl.ds(EXTRA, OWN), :] = value[:OWN]
        band_field[SOUTH, plane, tiles, pl.ds(0, OWN), :] = value[rows - OWN :]

    sides = Region(side_field, side_other, side_gain, side_scaled, side_coeff, 3, 3, 1)
    sides.closing_sides(sides.sweeps(starts), ends, smoothed, residual, targets, tiles - 1)

    for band, turned, landing, box_rows, target in ((SOUTH, bottom, OWN, lower, rows - 8), (NORTH, top, 0, upper, 0)):
        if band == NORTH:

            @pl.when(at_seam)
            def _():
                pl.semaphore_wait(north_in, 3)
                send_rows(NORTH, north, band_n, True)
                corners(NORTH, band_n, first_rows, ne, nw)

        for group, (planes, count) in enumerate(((slice(0, KLON), REACH), (slice(KLON, PLANES), REACH - 1))):
            got = rows_in.at[band, planes, pl.ds(0, count), :]
            pltpu.make_async_copy(got, got, row_recv.at[band, group]).wait()
        for slot, box in ((2 + 2 * band, east_in), (3 + 2 * band, west_in)):
            pltpu.make_async_copy(box.at[box_rows, :], box.at[box_rows, :], side_recv.at[slot]).wait()
        for plane in range(PLANES):
            band_field[band, plane, tiles, pl.ds(landing, 8), :] = unpacked(plane, east_in[box_rows, :], west_in[box_rows, :])

        def settle(order):
            def tile(t):
                columns = pl.ds(pl.multiple_of(t * LANES, LANES), LANES)
                band_field[band, :, t, pl.ds(landing, 8), :] = order(rows_in[band, :, :, columns])

            each_tile(tiles, tile)

        @pl.when(turned)
        def _():
            settle(flipped)
            block = band_field[band, :, tiles, pl.ds(landing, 8), :]
            band_field[band, :, tiles, pl.ds(landing, 8), :] = flipped(block)

        @pl.when(jnp.logical_not(turned))
        def _():
            settle(lambda block: block)

        edge = Region(
            band_field.at[band], band_other.at[band], band_gain.at[band], band_scaled.at[band], band_coeff.at[band], tiles + 1, BAND_UNROLL, BAND_END
        )
        edge.closing(edge.sweeps(chunks(4, OWN, BAND_CHUNK)), [(8, 8)], smoothed, residual, [target], tiles)

    for way in (SOUTH, NORTH):
        for group, (planes, count) in enumerate(((slice(0, KLON), REACH), (slice(KLON, PLANES), REACH - 1))):
            sent = rows_in.at[way, planes, pl.ds(0, count), :]
            pltpu.make_async_copy(sent, sent, row_send.at[way, group]).wait()
        for place, box in ((2 + 2 * way, to_east), (3 + 2 * way, to_west)):
            pltpu.make_async_copy(box.at[first_rows, :], box.at[first_rows, :], side_send.at[place]).wait()
    for place, box in ((0, to_east), (1, to_west)):
        pltpu.make_async_copy(box, box, side_send.at[place]).wait()


def solution(mesh):
    bands, sectors = mesh.shape["lat"], mesh.shape["lon"]

    def on_device(right_side, start, absorb, kappa_lat, kappa_lon):
        levels, rows, columns = start.shape
        tiles = columns // LANES + 1
        deep = rows + 16

        def region(tiles, *shape):
            return [
                pltpu.VMEM(lead + (tiles,) + shape[-1:] + (LANES,), jnp.float32)
                for lead in ((*shape[:-1], PLANES),) + ((*shape[:-1], 4),) * 4
            ]

        out = pltpu.VMEM(start.shape, jnp.float32)
        return pl.pallas_call(
            functools.partial(kernel, bands, sectors),
            out_shape=(out, out),
            in_specs=[pl.BlockSpec(memory_space=pltpu.HBM)] * 5,
            out_specs=[pl.BlockSpec(memory_space=pltpu.VMEM)] * 2,
            scratch_shapes=region(tiles - 1, deep) + region(tiles, 2, OWN + EXTRA) + region(3, deep) + [
                pltpu.VMEM((2, PLANES, 8, columns), jnp.float32),
                pltpu.VMEM((rows, LANES), jnp.float32),
                pltpu.VMEM((rows, LANES), jnp.float32),
                pltpu.VMEM((deep, LANES), jnp.float32),
                pltpu.VMEM((deep, LANES), jnp.float32),
                pltpu.SemaphoreType.DMA((tiles - 1,)),
                pltpu.SemaphoreType.DMA((4,)),
                pltpu.SemaphoreType.DMA((2, 2)),
                pltpu.SemaphoreType.DMA((2, 2)),
                pltpu.SemaphoreType.DMA((6,)),
                pltpu.SemaphoreType.DMA((6,)),
                pltpu.SemaphoreType.REGULAR,
            ],
            compiler_params=pltpu.CompilerParams(
                collective_id=0, has_side_effects=True, vmem_limit_bytes=62 * 1024 * 1024
            ),
        )(right_side, start, absorb, kappa_lat, kappa_lon)

    field = P(None, "lat", "lon")
    return jax.shard_map(
        on_device,
        mesh=mesh,
        in_specs=(field, field, field, P("lat", "lon"), P("lat", "lon")),
        out_specs=(field, field),
        check_vma=False,
    )
```
